1024 devices in a mesh: row: 16 (over x_hi, y, core), col: 64 (over x_lo, z).
Axes of the slice: x: 4 (x_hi: 2, x_lo: 2; x = x_hi * 2 + x_lo), y: 4, z: 32, core: 2. Of those that a mesh axis runs over, the one named last changes fastest.
Arguments:
- inputs: bfloat16 [1024, 6144], P('col', 'row'), may hold values from -6 to 6
- out_grad: bfloat16 [1024, 6144], P('col', 'row'), may hold values from -6 to 6
- w_first: bfloat16 [6144, 24576], P('row', 'col'), may hold values from -0.078125 to 0.078125
- w_second: bfloat16 [24576, 6144], P('col', 'row'), may hold values from -0.0390625 to 0.0390625
Outputs:
- d_input: bfloat16 [1024, 6144], P('col', 'row')
- grad_first: float32 [6144, 24576], P('row', 'col')
- grad_second: float32 [24576, 6144], P('col', 'row')
The draws below stay inside these ranges and needn't reach their ends.
All inputs are finite; a program needn't handle non-finite values.
Results may differ from the reference program's by a relative error of at most 0.0049.
Values may be sent and summed in bfloat16 or wider, within the bound.
No kernel may reach another device: no remote copies, remote signals or barrier semaphores. Data moves between devices by JAX's collectives and lax.ppermute only.
A program may use at most 32 MiB of HBM per device.

```python
import math
import jax
import jax.numpy as jnp
from jax import lax

D = 6144
FF = 24576
TOKENS = 1024


def steps_of(stream_key, dims, split, smallest, largest):
    def one(axis_at, parts):
        draws = jax.random.uniform(jax.random.fold_in(jax.random.fold_in(stream_key, 6), axis_at), (parts,), jnp.float32, smallest / len(split), largest / len(split))
        return jnp.repeat(jnp.exp(draws), dims[axis_at] // parts).reshape((-1,) + (1,) * (len(dims) - axis_at - 1))

    gain = one(*split[0])
    for cut in split[1:]:
        gain = gain * one(*cut)
    return gain


def scatter_about(stream_key, shape, deviation, reach, pieces=(), kind=jnp.bfloat16):
    drawn = deviation * jax.random.normal(stream_key, shape, jnp.float32)
    if pieces:
        drawn = drawn * steps_of(stream_key, shape, pieces, -0.22, 0.18)
    return jnp.clip(drawn, -reach, reach).astype(kind)


def setup_inputs(seed: int = 0) -> dict:
    keys = jax.random.split(jax.random.key(seed), 5)
    return {
        "inputs": scatter_about(keys[0], (TOKENS, D), 1.0, 6.0, ((0, 64), (1, 16))),
        "out_grad": scatter_about(keys[1], (TOKENS, D), 1.0, 6.0, ((0, 64), (1, 16))),
        "w_first": scatter_about(keys[2], (D, FF), D ** -0.5, 0.078125, ((0, 16), (1, 64))),
        "w_second": scatter_about(keys[3], (FF, D), FF ** -0.5, 0.0390625, ((0, 64), (1, 16))),
    }


def gelu_pair(pre):
    cdf = 0.5 * (1.0 + jax.scipy.special.erf(pre / math.sqrt(2.0)))
    dens = jnp.exp(-0.5 * pre * pre) / math.sqrt(2.0 * math.pi)
    return (pre * cdf, cdf + pre * dens)

def reference(inputs, out_grad, w_first, w_second):
    pre = jnp.dot(inputs, w_first, preferred_element_type=jnp.float32)
    back = lax.dot_general(out_grad, w_second, (((1,), (1,)), ((), ())), preferred_element_type=jnp.float32)
    value, slope = gelu_pair(pre)
    act = value.astype(jnp.bfloat16)
    d_pre = (back * slope).astype(jnp.bfloat16)
    grad_second = lax.dot_general(act, out_grad, (((0,), (0,)), ((), ())), preferred_element_type=jnp.float32)
    grad_first = lax.dot_general(inputs, d_pre, (((0,), (0,)), ((), ())), preferred_element_type=jnp.float32)
    d_input = lax.dot_general(d_pre, w_first, (((1,), (1,)), ((), ())), preferred_element_type=jnp.float32)
    return (d_input.astype(jnp.bfloat16), grad_first, grad_second)
```

```python
import math

import jax
import jax.numpy as jnp
from jax import lax
from jax.sharding import Mesh, PartitionSpec as P

ROW = ("xh", "y", "core")
NEAR = ("xl", "zl")
FAR = ("zh",)
F32 = jnp.float32
BF16 = jnp.bfloat16


def gelu_pair(pre):
    cdf = 0.5 * (1.0 + jax.scipy.special.erf(pre / math.sqrt(2.0)))
    dens = jnp.exp(-0.5 * pre * pre) / math.sqrt(2.0 * math.pi)
    return (pre * cdf, cdf + pre * dens)


def exchange(blocks, axes):
    return lax.all_to_all(blocks, axes, 0, 0, tiled=False)


def spread(block, axes, size):
    return exchange(jnp.broadcast_to(block[None], (size,) + block.shape), axes)


def local(inputs, out_grad, w_first, w_second):
    rows, width = inputs.shape
    pair = jnp.stack([inputs, out_grad])
    far = spread(pair, FAR, 8)
    far = far.transpose(1, 0, 2, 3).reshape(2, 8 * rows, width)
    near = spread(far, NEAR, 8)
    tokens = 64 * rows
    all_in = near[:, 0].reshape(tokens, width)
    all_grad = near[:, 1].reshape(tokens, width)
    pre_part = jnp.dot(all_in, w_first, preferred_element_type=F32)
    back_part = lax.dot_general(
        all_grad, w_second, (((1,), (1,)), ((), ())), preferred_element_type=F32
    )
    hidden = pre_part.shape[1]
    parts = jnp.concatenate([pre_part.astype(BF16), back_part.astype(BF16)], axis=1)
    parts = exchange(parts.reshape(16, tokens // 16, 2 * hidden), ROW)
    sums = jnp.sum(parts.astype(F32), axis=0)
    value, slope = gelu_pair(sums[:, :hidden])
    both = jnp.concatenate(
        [value.astype(BF16), (sums[:, hidden:] * slope).astype(BF16)], axis=1
    )
    both = spread(both, ROW, 16).reshape(tokens, 2 * hidden)
    act, d_pre = both[:, :hidden], both[:, hidden:]
    terms = lax.dot_general(
        d_pre, w_first, (((1,), (1,)), ((), ())), preferred_element_type=F32
    ).astype(BF16)
    terms = exchange(terms.reshape(8, 8 * rows, width), NEAR)
    terms = jnp.sum(terms.astype(F32), axis=0).astype(BF16)
    terms = exchange(terms.reshape(8, rows, width), FAR)
    d_input = jnp.sum(terms.astype(F32), axis=0).astype(BF16)
    grad_second = lax.dot_general(
        act, all_grad, (((0,), (0,)), ((), ())), preferred_element_type=F32
    )
    grad_first = lax.dot_general(
        all_in, d_pre, (((0,), (0,)), ((), ())), preferred_element_type=F32
    )
    return (d_input, grad_first, grad_second)


def solution(mesh):
    fine = Mesh(mesh.devices.reshape(2, 4, 2, 2, 8, 4), ("xh", "y", "core", "xl", "zh", "zl"))
    row, col = ROW, ("xl", "zh", "zl")
    placed = (P(col, row), P(col, row), P(row, col), P(col, row))
    return jax.shard_map(
        local,
        mesh=fine,
        in_specs=placed,
        out_specs=(P(col, row), P(row, col), P(col, row)),
        check_vma=False,
    )
```

```python
import math

import jax
import jax.numpy as jnp
from jax import lax
from jax.sharding import Mesh, PartitionSpec as P

QUAD = ("core", "xl")
PLANE = ("xh", "y")
FAR = ("core", "zh")
NEAR = ("zl",)
F32 = jnp.float32
BF16 = jnp.bfloat16


def gelu_pair(pre):
    cdf = 0.5 * (1.0 + jax.scipy.special.erf(pre / math.sqrt(2.0)))
    dens = jnp.exp(-0.5 * pre * pre) / math.sqrt(2.0 * math.pi)
    return (pre * cdf, cdf + pre * dens)


def exchange(blocks, axes):
    return lax.all_to_all(blocks, axes, 0, 0, tiled=False)


def flip(block, slab, column):
    return lax.ppermute(block, QUAD, [(i, i ^ (2 * slab + column)) for i in range(4)])


def dot(a, b, ca, cb):
    return lax.dot_general(a, b, (((ca,), (cb,)), ((), ())), preferred_element_type=F32)


def local(inputs, out_grad, w_first, w_second):
    rows, width = inputs.shape
    half = rows // 2
    core = lax.axis_index("core")

    packed = jnp.concatenate([w_first, w_second])
    held = [[packed, flip(packed, 0, 1)], [flip(packed, 1, 0), flip(packed, 1, 1)]]
    first = [[held[s][c][:width] for c in range(2)] for s in range(2)]
    second = [[held[s][c][width:] for c in range(2)] for s in range(2)]

    pair = jnp.stack([inputs, out_grad]).reshape(2, 2, half, width).transpose(1, 0, 2, 3)
    pair = jnp.broadcast_to(pair[:, None], (2, 8, 2, half, width))
    far = exchange(pair.reshape(16, 2, half, width), FAR).reshape(2, 8, 2, half, width)
    far = far.transpose(2, 0, 1, 3, 4).reshape(2, 2, 8 * half, width)
    own_in, own_grad = [jnp.where(core == 0, f[0], f[1]) for f in far]
    other_in, other_grad = [jnp.where(core == 0, f[1], f[0]) for f in far]
    far = jnp.concatenate([own_in, other_in, own_grad, other_grad], axis=1)
    near = lax.all_gather(far, NEAR, axis=0, tiled=True)
    tokens = near.shape[0]
    x = [near[:, s * width : (s + 1) * width] for s in range(2)]
    g = [near[:, (2 + s) * width : (3 + s) * width] for s in range(2)]

    pre = [dot(x[0], first[0][c], 1, 0) + dot(x[1], first[1][c], 1, 0) for c in range(2)]
    back = [dot(g[0], second[0][c], 1, 1) + dot(g[1], second[1][c], 1, 1) for c in range(2)]
    parts = jnp.concatenate([p.astype(BF16) for p in pre + back], axis=1)
    parts = exchange(parts.reshape(8, tokens // 8, 4 * width), PLANE)
    sums = jnp.sum(parts.astype(F32), axis=0)
    value, slope = gelu_pair(sums[:, : 2 * width])
    both = jnp.concatenate(
        [value.astype(BF16), (sums[:, 2 * width :] * slope).astype(BF16)], axis=1
    )
    both = exchange(jnp.broadcast_to(both[None], (8,) + both.shape), PLANE)
    both = both.reshape(tokens, 4 * width)
    act = [both[:, c * width : (c + 1) * width] for c in range(2)]
    d_pre = [both[:, (2 + c) * width : (3 + c) * width] for c in range(2)]

    terms = [dot(d_pre[0], first[s][0], 1, 1) + dot(d_pre[1], first[s][1], 1, 1) for s in range(2)]
    terms = jnp.concatenate([t.astype(BF16) for t in terms], axis=1)
    terms = exchange(terms.reshape(4, tokens // 4, 2 * width), NEAR)
    terms = jnp.sum(terms.astype(F32), axis=0).astype(BF16)
    own, other = terms[:, :width], terms[:, width:]
    terms = jnp.stack([jnp.where(core == 0, own, other), jnp.where(core == 0, other, own)])
    terms = exchange(terms.reshape(16, half, width), FAR).reshape(2, 8, half, width)
    d_input = jnp.sum(terms.astype(F32), axis=1).astype(BF16).reshape(rows, width)

    def grads(s, c):
        return (dot(x[s], d_pre[c], 0, 0), dot(act[c], g[s], 0, 0))

    grad_first, grad_second = grads(0, 0)
    for s, c in ((1, 0), (0, 1), (1, 1)):
        sent = jnp.concatenate([t.astype(BF16) for t in grads(s, c)])
        came = flip(sent, s, c).astype(F32)
        grad_first = grad_first + came[:width]
        grad_second = grad_second + came[width:]
    return (d_input, grad_first, grad_second)


def solution(mesh):
    fine = Mesh(mesh.devices.reshape(2, 4, 2, 2, 8, 4), ("xh", "y", "core", "xl", "zh", "zl"))
    row, col = ("xh", "y", "core"), ("xl", "zh", "zl")
    placed = (P(col, row), P(col, row), P(row, col), P(col, row))
    return jax.shard_map(
        local,
        mesh=fine,
        in_specs=placed,
        out_specs=(P(col, row), P(row, col), P(col, row)),
        check_vma=False,
    )
```

```python
import math

import jax
import jax.numpy as jnp
from jax import lax
from jax.sharding import Mesh, PartitionSpec as P

QUAD = ("core", "xl")
PLANE = ("xh", "y")
SPAN = ("core", "zh", "zl")
NEAR = ("zl",)
F32 = jnp.float32
BF16 = jnp.bfloat16


def gelu_pair(pre):
    cdf = 0.5 * (1.0 + jax.scipy.special.erf(pre / math.sqrt(2.0)))
    dens = jnp.exp(-0.5 * pre * pre) / math.sqrt(2.0 * math.pi)
    return (pre * cdf, cdf + pre * dens)


def exchange(blocks, axes):
    return lax.all_to_all(blocks, axes, 0, 0, tiled=False)


def exchange_far(blocks):
    groups = [
        [c * 32 + (z + 4) % 8 * 4 + low for c in range(2) for z in range(8)] for low in range(4)
    ]
    return lax.all_to_all(blocks, SPAN, 0, 0, axis_index_groups=groups, tiled=False)


def flip(block, slab, column):
    return lax.ppermute(block, QUAD, [(i, i ^ (2 * slab + column)) for i in range(4)])


def dot(a, b, ca, cb):
    return lax.dot_general(a, b, (((ca,), (cb,)), ((), ())), preferred_element_type=F32)


def local(inputs, out_grad, w_first, w_second):
    rows, width = inputs.shape
    half = rows // 2
    core = lax.axis_index("core")

    packed = jnp.concatenate([w_first, w_second])
    held = [[packed, flip(packed, 0, 1)], [flip(packed, 1, 0), flip(packed, 1, 1)]]
    first = [[held[s][c][:width] for c in range(2)] for s in range(2)]
    second = [[held[s][c][width:] for c in range(2)] for s in range(2)]

    pair = jnp.stack([inputs, out_grad]).reshape(2, 2, half, width).transpose(1, 0, 2, 3)
    pair = jnp.broadcast_to(pair[:, None], (2, 8, 2, half, width))
    far = exchange_far(pair.reshape(16, 2, half, width)).reshape(2, 8, 2, half, width)
    far = far.transpose(2, 0, 1, 3, 4).reshape(2, 2, 8 * half, width)
    own_in, own_grad = [jnp.where(core == 0, f[0], f[1]) for f in far]
    other_in, other_grad = [jnp.where(core == 0, f[1], f[0]) for f in far]
    far = jnp.concatenate([own_in, other_in, own_grad, other_grad], axis=1)
    near = lax.all_gather(far, NEAR, axis=0, tiled=True)
    tokens = near.shape[0]
    x = [near[:, s * width : (s + 1) * width] for s in range(2)]
    g = [near[:, (2 + s) * width : (3 + s) * width] for s in range(2)]

    pre = [dot(x[0], first[0][c], 1, 0) + dot(x[1], first[1][c], 1, 0) for c in range(2)]
    back = [dot(g[0], second[0][c], 1, 1) + dot(g[1], second[1][c], 1, 1) for c in range(2)]
    parts = jnp.concatenate([p.astype(BF16) for p in pre + back], axis=1)
    parts = exchange(parts.reshape(8, tokens // 8, 4 * width), PLANE)
    sums = jnp.sum(parts.astype(F32), axis=0)
    value, slope = gelu_pair(sums[:, : 2 * width])
    both = jnp.concatenate(
        [value.astype(BF16), (sums[:, 2 * width :] * slope).astype(BF16)], axis=1
    )
    both = exchange(jnp.broadcast_to(both[None], (8,) + both.shape), PLANE)
    both = both.reshape(tokens, 4 * width)
    act = [both[:, c * width : (c + 1) * width] for c in range(2)]
    d_pre = [both[:, (2 + c) * width : (3 + c) * width] for c in range(2)]

    terms = [dot(d_pre[0], first[s][0], 1, 1) + dot(d_pre[1], first[s][1], 1, 1) for s in range(2)]
    terms = jnp.concatenate([t.astype(BF16) for t in terms], axis=1)

    def grads(s, c):
        return [dot(x[s], d_pre[c], 0, 0), dot(act[c], g[s], 0, 0)]

    sent = jnp.concatenate([t.astype(BF16) for c in range(2) for t in grads(1, c)])
    terms, sent = lax.optimization_barrier((terms, sent))
    came = flip(sent, 1, 0).reshape(2, 2, width, width).astype(F32)
    kept = [[t + came[c, i] for i, t in enumerate(grads(0, c))] for c in range(2)]
    mixed = jnp.concatenate([t.astype(BF16) for t in kept[1]])

    terms = exchange(terms.reshape(4, tokens // 4, 2 * width), NEAR)
    terms = jnp.sum(terms.astype(F32), axis=0).astype(BF16)
    own, other = terms[:, :width], terms[:, width:]
    terms = jnp.stack([jnp.where(core == 0, own, other), jnp.where(core == 0, other, own)])
    terms = exchange_far(terms.reshape(16, half, width)).reshape(2, 8, half, width)
    d_input = jnp.sum(terms.astype(F32), axis=1).astype(BF16).reshape(rows, width)

    came = flip(mixed, 0, 1)
    grad_first = kept[0][0] + came[:width].astype(F32)
    grad_second = kept[0][1] + came[width:].astype(F32)
    return (d_input, grad_first, grad_second)


def solution(mesh):
    fine = Mesh(mesh.devices.reshape(2, 4, 2, 2, 8, 4), ("xh", "y", "core", "xl", "zh", "zl"))
    row, col = ("xh", "y", "core"), ("xl", "zh", "zl")
    placed = (P(col, row), P(col, row), P(row, col), P(col, row))
    return jax.shard_map(
        local,
        mesh=fine,
        in_specs=placed,
        out_specs=(P(col, row), P(row, col), P(col, row)),
        check_vma=False,
    )
```

```python
import functools
import math

import jax
import jax.numpy as jnp
from jax import lax
from jax.experimental import pallas as pl
from jax.experimental.pallas import tpu as pltpu
from jax.sharding import Mesh, PartitionSpec as P

QUAD = ("core", "xl")
PLANE = ("xh", "y")
LIMIT = 16
COST = pl.CostEstimate(flops=30 * 10**9, bytes_accessed=2**22, transcendentals=0)
BOUND = pl.CostEstimate(flops=10**9, bytes_accessed=2**10, transcendentals=0)
SPAN = ("core", "zh", "zl")
NEAR = ("zl",)
F32 = jnp.float32
BF16 = jnp.bfloat16


def gelu_pair(pre):
    cdf = 0.5 * (1.0 + jax.scipy.special.erf(pre / math.sqrt(2.0)))
    dens = jnp.exp(-0.5 * pre * pre) / math.sqrt(2.0 * math.pi)
    return (pre * cdf, cdf + pre * dens)


def exchange(blocks, axes):
    return lax.all_to_all(blocks, axes, 0, 0, tiled=False)


def exchange_far(blocks):
    groups = [
        [c * 32 + z * 4 + low for z in (4, 0, 1, 7, 2, 6, 3, 5) for c in range(2)] for low in range(4)
    ]
    return lax.all_to_all(blocks, SPAN, 0, 0, axis_index_groups=groups, tiled=False)


def flip(block, slab, column):
    return lax.ppermute(block, QUAD, [(i, i ^ (2 * slab + column)) for i in range(4)])


def dot(a, b, ca, cb):
    return lax.dot_general(a, b, (((ca,), (cb,)), ((), ())), preferred_element_type=F32)


def call(kernel, outs, *operands, scalars=0, far=0, cost=None):
    specs = [pl.BlockSpec(memory_space=pltpu.SMEM)] * scalars
    specs += [pl.BlockSpec(memory_space=pltpu.VMEM)] * (len(operands) - scalars)
    out_specs = [pl.BlockSpec(memory_space=pltpu.HBM)] * far
    out_specs += [pl.BlockSpec(memory_space=pltpu.VMEM)] * (len(outs) - far)
    scratch = [pltpu.VMEM(shape, kind) for shape, kind in outs[:far]]
    scratch += [pltpu.SemaphoreType.DMA] * far
    return pl.pallas_call(
        kernel,
        out_shape=[jax.ShapeDtypeStruct(shape, kind) for shape, kind in outs],
        in_specs=specs,
        out_specs=out_specs,
        scratch_shapes=scratch,
        cost_estimate=cost,
        compiler_params=pltpu.CompilerParams(vmem_limit_bytes=LIMIT * 2**20),
    )(*operands)


def act_kernel(parts, out, held, done):
    half = parts.shape[2] // 2
    sums = parts[0].astype(F32)
    for i in range(1, 8):
        sums += parts[i].astype(F32)
    value, slope = gelu_pair(sums[:, :half])
    value = value.astype(BF16)
    slope = (sums[:, half:] * slope).astype(BF16)
    for i in range(8):
        held[i, :, :half] = value
        held[i, :, half:] = slope
    copy = pltpu.make_async_copy(held, out, done)
    copy.start()
    copy.wait()


def sum_kernel(terms, out, held, done):
    sums = terms[0].astype(F32)
    for i in range(1, 4):
        sums += terms[i].astype(F32)
    width = sums.shape[1] // 2
    for a in range(2):
        held[:, a] = sums[:, a * width : (a + 1) * width].reshape(8, 8, width).astype(BF16)
    copy = pltpu.make_async_copy(held, out, done)
    copy.start()
    copy.wait()


def forward_kernel(*refs):
    pieces, (w00, w01, w10, w11, near, parts) = refs[:-6], refs[-6:]
    at = 0
    for piece in pieces:
        near[at : at + piece.shape[0]] = piece[...]
        at += piece.shape[0]
    width = w00.shape[1]
    for c, (own, other) in enumerate(((w00, w10), (w01, w11))):
        for j in range(2):
            rows, contract = slice(j * width, (j + 1) * width), j
            sums = dot(near[:, 2 * j * width : (2 * j + 1) * width], own[rows], 1, contract)
            sums += dot(near[:, (2 * j + 1) * width : (2 * j + 2) * width], other[rows], 1, contract)
            parts[:, (2 * j + c) * width : (2 * j + c + 1) * width] = sums.astype(BF16)


def terms_kernel(core, both, w00, w01, w10, w11, terms, held, done):
    width = w00.shape[1]
    d = [both[:, (2 + c) * width : (3 + c) * width] for c in range(2)]
    slabs = [
        dot(d[0], row[0][:width], 1, 1) + dot(d[1], row[1][:width], 1, 1)
        for row in ((w00, w01), (w10, w11))
    ]
    for a in range(2):
        chosen = jnp.where(core[0] == a, slabs[0], slabs[1]).astype(BF16)
        held[:, :, a * width : (a + 1) * width] = chosen.reshape(4, 64, width)
    copy = pltpu.make_async_copy(held, terms, done)
    copy.start()
    copy.wait()


def two_grads(near, both, slab, column):
    width = both.shape[1] // 4
    part = lambda ref, i: ref[:, i * width : (i + 1) * width]
    return (
        dot(part(near, slab), part(both, 2 + column), 0, 0),
        dot(part(both, column), part(near, 2 + slab), 0, 0),
    )


def send_kernel(slab, column, near, both, sent):
    width = sent.shape[1]
    first, second = two_grads(near, both, slab, column)
    sent[:width] = first.astype(BF16)
    sent[width:] = second.astype(BF16)


def grads_kernel(near, both, came0, came1, came2, grad_first, grad_second):
    width = grad_first.shape[0]
    first, second = two_grads(near, both, 0, 0)
    for came in (came0, came1, came2):
        first += came[:width].astype(F32)
        second += came[width:].astype(F32)
    grad_first[...] = first
    grad_second[...] = second


def local(inputs, out_grad, w_first, w_second):
    rows, width = inputs.shape
    half = rows // 2
    core = lax.axis_index("core")

    packed = jnp.concatenate([w_first, w_second])
    held = [packed, flip(packed, 0, 1), flip(packed, 1, 0), flip(packed, 1, 1)]

    pair = jnp.stack([inputs, out_grad]).reshape(2, 2, half, width).transpose(1, 0, 2, 3)
    pair = jnp.broadcast_to(pair[None], (8, 2, 2, half, width))
    far = exchange_far(pair.reshape(16, 2, half, width)).reshape(8, 2, 2, half, width)
    far = far.transpose(2, 1, 0, 3, 4).reshape(2, 2, 8 * half, width)
    own_in, own_grad = [jnp.where(core == 0, f[0], f[1]) for f in far]
    other_in, other_grad = [jnp.where(core == 0, f[1], f[0]) for f in far]
    far = jnp.concatenate([own_in, other_in, own_grad, other_grad], axis=1)

    pieces = [lax.all_gather(far, NEAR, axis=0, tiled=True)]
    tokens = 32 * half
    near, parts = call(
        forward_kernel,
        [((tokens, 4 * width), BF16), ((tokens, 4 * width), BF16)],
        *pieces,
        *held,
    )
    parts = exchange(parts.reshape(8, tokens // 8, 4 * width), PLANE)
    (both,) = call(act_kernel, [(parts.shape, BF16)], parts, far=1)
    both = exchange(both, PLANE)
    both = both.reshape(tokens, 4 * width)

    (terms,) = call(
        terms_kernel,
        [((4, 8 * half, 2 * width), BF16)],
        core.reshape(1).astype(jnp.int32),
        both,
        *held,
        scalars=1,
        far=1,
        cost=BOUND,
    )
    ways = ((1, 1), (0, 1), (1, 0))
    sent = [
        call(
            functools.partial(send_kernel, s, c),
            [((2 * width, width), BF16)],
            near,
            both,
            cost=BOUND,
        )[0]
        for s, c in ways
    ]
    came = [flip(block, s, c) for block, (s, c) in zip(sent, ways)]
    terms = exchange(terms, NEAR)
    (terms,) = call(sum_kernel, [((8, 2, half, width), BF16)], terms, far=1)
    terms = exchange_far(terms.reshape(16, half, width)).reshape(8, 2, half, width)
    d_input = jnp.sum(terms.astype(F32), axis=0).astype(BF16).reshape(rows, width)
    grad_first, grad_second = call(grads_kernel, [((width, width), F32)] * 2, near, both, *came, cost=COST)
    return (d_input, grad_first, grad_second)


def solution(mesh):
    fine = Mesh(mesh.devices.reshape(2, 4, 2, 2, 8, 4), ("xh", "y", "core", "xl", "zh", "zl"))
    row, col = ("xh", "y", "core"), ("xl", "zh", "zl")
    placed = (P(col, row), P(col, row), P(row, col), P(col, row))
    return jax.shard_map(
        local,
        mesh=fine,
        in_specs=placed,
        out_specs=(P(col, row), P(row, col), P(col, row)),
        check_vma=False,
    )
```

```python
import math

import jax
import jax.numpy as jnp
from jax import lax
from jax.experimental import pallas as pl
from jax.experimental.pallas import tpu as pltpu
from jax.sharding import Mesh, PartitionSpec as P

QUAD = ("core", "xl")
PLANE = ("xh", "y")
LIMIT = 16
COST = pl.CostEstimate(flops=30 * 10**9, bytes_accessed=2**22, transcendentals=0)
BOUND = pl.CostEstimate(flops=10**9, bytes_accessed=2**10, transcendentals=0)
SPAN = ("core", "zh", "zl")
NEAR = ("zl",)
WAYS = ((1, 1), (0, 1), (1, 0))
F32 = jnp.float32
BF16 = jnp.bfloat16


def gelu_pair(pre):
    cdf = 0.5 * (1.0 + jax.scipy.special.erf(pre / math.sqrt(2.0)))
    dens = jnp.exp(-0.5 * pre * pre) / math.sqrt(2.0 * math.pi)
    return (pre * cdf, cdf + pre * dens)


def exchange(blocks, axes):
    return lax.all_to_all(blocks, axes, 0, 0, tiled=False)


def exchange_far(blocks):
    groups = [
        [c * 32 + z * 4 + low for z in (4, 0, 1, 7, 2, 6, 3, 5) for c in range(2)] for low in range(4)
    ]
    return lax.all_to_all(blocks, SPAN, 0, 0, axis_index_groups=groups, tiled=False)


def flip(block, slab, column):
    return lax.ppermute(block, QUAD, [(i, i ^ (2 * slab + column)) for i in range(4)])


def dot(a, b, ca, cb):
    return lax.dot_general(a, b, (((ca,), (cb,)), ((), ())), preferred_element_type=F32)


def call(kernel, outs, *operands, scalars=0, far=0, cost=None, limit=LIMIT):
    specs = [pl.BlockSpec(memory_space=pltpu.SMEM)] * scalars
    specs += [pl.BlockSpec(memory_space=pltpu.VMEM)] * (len(operands) - scalars)
    out_specs = [pl.BlockSpec(memory_space=pltpu.HBM)] * far
    out_specs += [pl.BlockSpec(memory_space=pltpu.VMEM)] * (len(outs) - far)
    scratch = [pltpu.VMEM(shape, kind) for shape, kind in outs[:far]]
    scratch += [pltpu.SemaphoreType.DMA] * far
    return pl.pallas_call(
        kernel,
        out_shape=[jax.ShapeDtypeStruct(shape, kind) for shape, kind in outs],
        in_specs=specs,
        out_specs=out_specs,
        scratch_shapes=scratch,
        cost_estimate=cost,
        compiler_params=pltpu.CompilerParams(vmem_limit_bytes=limit * 2**20),
    )(*operands)


def spread_kernel(inputs, out_grad, out, held, done):
    half = inputs.shape[0] // 2
    for i, block in enumerate((inputs, out_grad)):
        wide = block[...].astype(F32)
        for c in range(2):
            piece = wide[c * half : (c + 1) * half].astype(BF16)
            for k in range(8):
                held[k, c, i] = piece
    copy = pltpu.make_async_copy(held, out, done)
    copy.start()
    copy.wait()


def act_kernel(parts, out, held, done):
    half = parts.shape[2] // 2
    sums = parts[0].astype(F32)
    for i in range(1, 8):
        sums += parts[i].astype(F32)
    value, slope = gelu_pair(sums[:, :half])
    value = value.astype(BF16)
    slope = (sums[:, half:] * slope).astype(BF16)
    for i in range(8):
        held[i, :, :half] = value
        held[i, :, half:] = slope
    copy = pltpu.make_async_copy(held, out, done)
    copy.start()
    copy.wait()


def sum_kernel(terms, out, held, done):
    sums = terms[0].astype(F32)
    for i in range(1, 4):
        sums += terms[i].astype(F32)
    width = sums.shape[1] // 2
    for a in range(2):
        held[:, a] = sums[:, a * width : (a + 1) * width].reshape(8, 8, width).astype(BF16)
    copy = pltpu.make_async_copy(held, out, done)
    copy.start()
    copy.wait()


def forward_kernel(*refs):
    pieces, (w00, w01, w10, w11, near, parts) = refs[:-6], refs[-6:]
    at = 0
    for piece in pieces:
        near[at : at + piece.shape[0]] = piece[...]
        at += piece.shape[0]
    width = w00.shape[1]
    for c, (own, other) in enumerate(((w00, w10), (w01, w11))):
        for j in range(2):
            rows, contract = slice(j * width, (j + 1) * width), j
            sums = dot(near[:, 2 * j * width : (2 * j + 1) * width], own[rows], 1, contract)
            sums += dot(near[:, (2 * j + 1) * width : (2 * j + 2) * width], other[rows], 1, contract)
            parts[:, (2 * j + c) * width : (2 * j + c + 1) * width] = sums.astype(BF16)


def terms_kernel(core, both, w00, w01, w10, w11, terms, held, done):
    width = w00.shape[1]
    d = [both[:, (2 + c) * width : (3 + c) * width] for c in range(2)]
    slabs = [
        dot(d[0], row[0][:width], 1, 1) + dot(d[1], row[1][:width], 1, 1)
        for row in ((w00, w01), (w10, w11))
    ]
    for a in range(2):
        chosen = jnp.where(core[0] == a, slabs[0], slabs[1]).astype(BF16)
        held[:, :, a * width : (a + 1) * width] = chosen.reshape(4, 64, width)
    copy = pltpu.make_async_copy(held, terms, done)
    copy.start()
    copy.wait()


def two_grads(near, both, slab, column):
    width = both.shape[1] // 4
    part = lambda ref, i: ref[:, i * width : (i + 1) * width]
    return (
        dot(part(near, slab), part(both, 2 + column), 0, 0),
        dot(part(both, column), part(near, 2 + slab), 0, 0),
    )


def send_kernel(near, both, out0, out1, out2, held0, held1, held2, done0, done1, done2):
    width = out0.shape[1]
    copies = []
    for (slab, column), out, held, done in zip(
        WAYS, (out0, out1, out2), (held0, held1, held2), (done0, done1, done2)
    ):
        first, second = two_grads(near, both, slab, column)
        held[:width] = first.astype(BF16)
        held[width:] = second.astype(BF16)
        copies.append(pltpu.make_async_copy(held, out, done))
        copies[-1].start()
    for copy in copies:
        copy.wait()


def grads_kernel(near, both, came0, came1, came2, grad_first, grad_second):
    width = grad_first.shape[0]
    first, second = two_grads(near, both, 0, 0)
    for came in (came0, came1, came2):
        first += came[:width].astype(F32)
        second += came[width:].astype(F32)
    grad_first[...] = first
    grad_second[...] = second


def local(inputs, out_grad, w_first, w_second):
    rows, width = inputs.shape
    half = rows // 2
    core = lax.axis_index("core")

    packed = jnp.concatenate([w_first, w_second])
    held = [packed, flip(packed, 0, 1), flip(packed, 1, 0), flip(packed, 1, 1)]

    blocks = [((8, 2, 2, half, width), BF16)]
    (pair,) = call(spread_kernel, blocks, inputs, out_grad, far=1, limit=56)
    far = exchange_far(pair.reshape(16, 2, half, width)).reshape(8, 2, 2, half, width)
    far = far.transpose(2, 1, 0, 3, 4).reshape(2, 2, 8 * half, width)
    own_in, own_grad = [jnp.where(core == 0, f[0], f[1]) for f in far]
    other_in, other_grad = [jnp.where(core == 0, f[1], f[0]) for f in far]
    far = jnp.concatenate([own_in, other_in, own_grad, other_grad], axis=1)

    pieces = [lax.all_gather(far, NEAR, axis=0, tiled=True)]
    tokens = 32 * half
    near, parts = call(
        forward_kernel,
        [((tokens, 4 * width), BF16), ((tokens, 4 * width), BF16)],
        *pieces,
        *held,
    )
    parts = exchange(parts.reshape(8, tokens // 8, 4 * width), PLANE)
    (both,) = call(act_kernel, [(parts.shape, BF16)], parts, far=1)
    both = exchange(both, PLANE)
    both = both.reshape(tokens, 4 * width)

    (terms,) = call(
        terms_kernel,
        [((4, 8 * half, 2 * width), BF16)],
        core.reshape(1).astype(jnp.int32),
        both,
        *held,
        scalars=1,
        far=1,
        cost=BOUND,
    )
    blocks = [((2 * width, width), BF16)] * 3
    sent = call(send_kernel, blocks, near, both, far=3, cost=BOUND)
    came = [flip(block, *way) for block, way in zip(sent, WAYS)]
    terms = exchange(terms, NEAR)
    (terms,) = call(sum_kernel, [((8, 2, half, width), BF16)], terms, far=1)
    terms = exchange_far(terms.reshape(16, half, width)).reshape(8, 2, half, width)
    d_input = jnp.sum(terms.astype(F32), axis=0).astype(BF16).reshape(rows, width)
    grad_first, grad_second = call(grads_kernel, [((width, width), F32)] * 2, near, both, *came, cost=COST)
    return (d_input, grad_first, grad_second)


def solution(mesh):
    fine = Mesh(mesh.devices.reshape(2, 4, 2, 2, 8, 4), ("xh", "y", "core", "xl", "zh", "zl"))
    row, col = ("xh", "y", "core"), ("xl", "zh", "zl")
    placed = (P(col, row), P(col, row), P(row, col), P(col, row))
    return jax.shard_map(
        local,
        mesh=fine,
        in_specs=placed,
        out_specs=(P(col, row), P(row, col), P(col, row)),
        check_vma=False,
    )
```

```python
import math

import jax
import jax.numpy as jnp
from jax import lax
from jax.experimental import pallas as pl
from jax.experimental.pallas import tpu as pltpu
from jax.sharding import Mesh, PartitionSpec as P

QUAD = ("core", "xl")
PLANE = ("xh", "y")
LIMIT = 16
COST = pl.CostEstimate(flops=30 * 10**9, bytes_accessed=2**22, transcendentals=0)
BOUND = pl.CostEstimate(flops=10**9, bytes_accessed=2**10, transcendentals=0)
SPAN = ("core", "zh", "zl")
RING = ("zh", "zl")
FOLD = [[z * 4 + low for low in (1, 0, 2, 3)] for z in range(8)]
WAYS = ((1, 1), (0, 1), (1, 0))
F32 = jnp.float32
BF16 = jnp.bfloat16


def gelu_pair(pre):
    cdf = 0.5 * (1.0 + jax.scipy.special.erf(pre / math.sqrt(2.0)))
    dens = jnp.exp(-0.5 * pre * pre) / math.sqrt(2.0 * math.pi)
    return (pre * cdf, cdf + pre * dens)


def exchange(blocks, axes):
    return lax.all_to_all(blocks, axes, 0, 0, tiled=False)


def exchange_far(blocks):
    groups = [
        [c * 32 + z * 4 + low for z in (4, 0, 1, 7, 2, 6, 3, 5) for c in range(2)] for low in range(4)
    ]
    return lax.all_to_all(blocks, SPAN, 0, 0, axis_index_groups=groups, tiled=False)


def flip(block, slab, column):
    return lax.ppermute(block, QUAD, [(i, i ^ (2 * slab + column)) for i in range(4)])


def dot(a, b, ca, cb):
    return lax.dot_general(a, b, (((ca,), (cb,)), ((), ())), preferred_element_type=F32)


def call(kernel, outs, *operands, scalars=0, far=0, cost=None, limit=LIMIT):
    specs = [pl.BlockSpec(memory_space=pltpu.SMEM)] * scalars
    specs += [pl.BlockSpec(memory_space=pltpu.VMEM)] * (len(operands) - scalars)
    out_specs = [pl.BlockSpec(memory_space=pltpu.HBM)] * far
    out_specs += [pl.BlockSpec(memory_space=pltpu.VMEM)] * (len(outs) - far)
    scratch = [pltpu.VMEM(shape, kind) for shape, kind in outs[:far]]
    scratch += [pltpu.SemaphoreType.DMA] * far
    return pl.pallas_call(
        kernel,
        out_shape=[jax.ShapeDtypeStruct(shape, kind) for shape, kind in outs],
        in_specs=specs,
        out_specs=out_specs,
        scratch_shapes=scratch,
        cost_estimate=cost,
        compiler_params=pltpu.CompilerParams(vmem_limit_bytes=limit * 2**20),
    )(*operands)


def spread_kernel(inputs, out_grad, out, held, done):
    half = inputs.shape[0] // 2
    for i, block in enumerate((inputs, out_grad)):
        wide = block[...].astype(F32)
        for c in range(2):
            piece = wide[c * half : (c + 1) * half].astype(BF16)
            for k in range(8):
                held[k, c, i] = piece
    copy = pltpu.make_async_copy(held, out, done)
    copy.start()
    copy.wait()


def act_kernel(parts, out, held, done):
    half = parts.shape[2] // 2
    sums = parts[0].astype(F32)
    for i in range(1, 8):
        sums += parts[i].astype(F32)
    value, slope = gelu_pair(sums[:, :half])
    value = value.astype(BF16)
    slope = (sums[:, half:] * slope).astype(BF16)
    for i in range(8):
        held[i, :, :half] = value
        held[i, :, half:] = slope
    copy = pltpu.make_async_copy(held, out, done)
    copy.start()
    copy.wait()


def sum_kernel(terms, out, held, done):
    sums = terms[0].astype(F32)
    for i in range(1, 4):
        sums += terms[i].astype(F32)
    width = sums.shape[1] // 2
    for a in range(2):
        held[:, a] = sums[:, a * width : (a + 1) * width].reshape(8, 8, width).astype(BF16)
    copy = pltpu.make_async_copy(held, out, done)
    copy.start()
    copy.wait()


def forward_kernel(*refs):
    pieces, (w00, w01, w10, w11, near, parts) = refs[:-6], refs[-6:]
    at = 0
    for piece in pieces:
        near[at : at + piece.shape[0]] = piece[...]
        at += piece.shape[0]
    width = w00.shape[1]
    for c, (own, other) in enumerate(((w00, w10), (w01, w11))):
        for j in range(2):
            rows, contract = slice(j * width, (j + 1) * width), j
            sums = dot(near[:, 2 * j * width : (2 * j + 1) * width], own[rows], 1, contract)
            sums += dot(near[:, (2 * j + 1) * width : (2 * j + 2) * width], other[rows], 1, contract)
            parts[:, (2 * j + c) * width : (2 * j + c + 1) * width] = sums.astype(BF16)


def terms_kernel(core, both, w00, w01, w10, w11, terms, held, done):
    width = w00.shape[1]
    d = [both[:, (2 + c) * width : (3 + c) * width] for c in range(2)]
    slabs = [
        dot(d[0], row[0][:width], 1, 1) + dot(d[1], row[1][:width], 1, 1)
        for row in ((w00, w01), (w10, w11))
    ]
    for a in range(2):
        chosen = jnp.where(core[0] == a, slabs[0], slabs[1]).astype(BF16)
        held[:, :, a * width : (a + 1) * width] = chosen.reshape(4, 64, width)
    copy = pltpu.make_async_copy(held, terms, done)
    copy.start()
    copy.wait()


def two_grads(near, both, slab, column):
    width = both.shape[1] // 4
    part = lambda ref, i: ref[:, i * width : (i + 1) * width]
    return (
        dot(part(near, slab), part(both, 2 + column), 0, 0),
        dot(part(both, column), part(near, 2 + slab), 0, 0),
    )


def send_kernel(near, both, out0, out1, out2, held0, held1, held2, done0, done1, done2):
    width = out0.shape[1]
    copies = []
    for (slab, column), out, held, done in zip(
        WAYS, (out0, out1, out2), (held0, held1, held2), (done0, done1, done2)
    ):
        first, second = two_grads(near, both, slab, column)
        held[:width] = first.astype(BF16)
        held[width:] = second.astype(BF16)
        copies.append(pltpu.make_async_copy(held, out, done))
        copies[-1].start()
    for copy in copies:
        copy.wait()


def grads_kernel(near, both, came0, came1, came2, grad_first, grad_second):
    width = grad_first.shape[0]
    first, second = two_grads(near, both, 0, 0)
    for came in (came0, came1, came2):
        first += came[:width].astype(F32)
        second += came[width:].astype(F32)
    grad_first[...] = first
    grad_second[...] = second


def local(inputs, out_grad, w_first, w_second):
    rows, width = inputs.shape
    half = rows // 2
    core = lax.axis_index("core")

    packed = jnp.concatenate([w_first, w_second])
    held = [packed, flip(packed, 0, 1), flip(packed, 1, 0), flip(packed, 1, 1)]

    blocks = [((8, 2, 2, half, width), BF16)]
    (pair,) = call(spread_kernel, blocks, inputs, out_grad, far=1, limit=56)
    far = exchange_far(pair.reshape(16, 2, half, width)).reshape(8, 2, 2, half, width)
    far = far.transpose(2, 1, 0, 3, 4).reshape(2, 2, 8 * half, width)
    own_in, own_grad = [jnp.where(core == 0, f[0], f[1]) for f in far]
    other_in, other_grad = [jnp.where(core == 0, f[1], f[0]) for f in far]
    far = jnp.concatenate([own_in, other_in, own_grad, other_grad], axis=1)

    pieces = [lax.all_gather(far, RING, axis=0, axis_index_groups=FOLD, tiled=True)]
    tokens = 32 * half
    near, parts = call(
        forward_kernel,
        [((tokens, 4 * width), BF16), ((tokens, 4 * width), BF16)],
        *pieces,
        *held,
    )
    parts = exchange(parts.reshape(8, tokens // 8, 4 * width), PLANE)
    (both,) = call(act_kernel, [(parts.shape, BF16)], parts, far=1)
    both = exchange(both, PLANE)
    both = both.reshape(tokens, 4 * width)

    (terms,) = call(
        terms_kernel,
        [((4, 8 * half, 2 * width), BF16)],
        core.reshape(1).astype(jnp.int32),
        both,
        *held,
        scalars=1,
        far=1,
        cost=BOUND,
    )
    blocks = [((2 * width, width), BF16)] * 3
    sent = call(send_kernel, blocks, near, both, far=3, cost=BOUND)
    came = [flip(block, *way) for block, way in zip(sent, WAYS)]
    terms = lax.all_to_all(terms, RING, 0, 0, axis_index_groups=FOLD, tiled=False)
    (terms,) = call(sum_kernel, [((8, 2, half, width), BF16)], terms, far=1)
    terms = exchange_far(terms.reshape(16, half, width)).reshape(8, 2, half, width)
    d_input = jnp.sum(terms.astype(F32), axis=0).astype(BF16).reshape(rows, width)
    grad_first, grad_second = call(grads_kernel, [((width, width), F32)] * 2, near, both, *came, cost=COST)
    return (d_input, grad_first, grad_second)


def solution(mesh):
    fine = Mesh(mesh.devices.reshape(2, 4, 2, 2, 8, 4), ("xh", "y", "core", "xl", "zh", "zl"))
    row, col = ("xh", "y", "core"), ("xl", "zh", "zl")
    placed = (P(col, row), P(col, row), P(row, col), P(col, row))
    return jax.shard_map(
        local,
        mesh=fine,
        in_specs=placed,
        out_specs=(P(col, row), P(row, col), P(col, row)),
        check_vma=False,
    )
```

```python
import math

import jax
import jax.numpy as jnp
from jax import lax
from jax.experimental import pallas as pl
from jax.experimental.pallas import tpu as pltpu
from jax.sharding import Mesh, PartitionSpec as P

QUAD = ("core", "xl")
PLANE = ("xh", "y")
LIMIT = 16
COST = pl.CostEstimate(flops=30 * 10**9, bytes_accessed=2**22, transcendentals=0)
BOUND = pl.CostEstimate(flops=10**9, bytes_accessed=2**10, transcendentals=0)
SPAN = ("core", "zh", "zl")
RING = ("zh", "zl")
FOLD = [[z * 4 + low for low in (1, 0, 2, 3)] for z in range(8)]
WAYS = ((1, 1), (0, 1), (1, 0))
F32 = jnp.float32
BF16 = jnp.bfloat16


def gelu_pair(pre):
    cdf = 0.5 * (1.0 + jax.scipy.special.erf(pre / math.sqrt(2.0)))
    dens = jnp.exp(-0.5 * pre * pre) / math.sqrt(2.0 * math.pi)
    return (pre * cdf, cdf + pre * dens)


def exchange(blocks, axes):
    return lax.all_to_all(blocks, axes, 0, 0, tiled=False)


def exchange_far(blocks):
    groups = [
        [c * 32 + z * 4 + low for z in (4, 0, 1, 7, 2, 6, 3, 5) for c in range(2)] for low in range(4)
    ]
    return lax.all_to_all(blocks, SPAN, 0, 0, axis_index_groups=groups, tiled=False)


def flip(block, slab, column):
    return lax.ppermute(block, QUAD, [(i, i ^ (2 * slab + column)) for i in range(4)])


def dot(a, b, ca, cb):
    return lax.dot_general(a, b, (((ca,), (cb,)), ((), ())), preferred_element_type=F32)


def call(kernel, outs, *operands, scalars=0, far=0, cost=None, limit=LIMIT):
    specs = [pl.BlockSpec(memory_space=pltpu.SMEM)] * scalars
    specs += [pl.BlockSpec(memory_space=pltpu.VMEM)] * (len(operands) - scalars)
    out_specs = [pl.BlockSpec(memory_space=pltpu.HBM)] * far
    out_specs += [pl.BlockSpec(memory_space=pltpu.VMEM)] * (len(outs) - far)
    scratch = [pltpu.VMEM(shape, kind) for shape, kind in outs[:far]]
    scratch += [pltpu.SemaphoreType.DMA] * far
    return pl.pallas_call(
        kernel,
        out_shape=[jax.ShapeDtypeStruct(shape, kind) for shape, kind in outs],
        in_specs=specs,
        out_specs=out_specs,
        scratch_shapes=scratch,
        cost_estimate=cost,
        compiler_params=pltpu.CompilerParams(vmem_limit_bytes=limit * 2**20),
    )(*operands)


def spread_kernel(inputs, out_grad, out, held, done):
    half = inputs.shape[0] // 2
    for i, block in enumerate((inputs, out_grad)):
        wide = block[...].astype(F32)
        for c in range(2):
            piece = wide[c * half : (c + 1) * half].astype(BF16)
            for k in range(8):
                held[k, c, i] = piece
    copy = pltpu.make_async_copy(held, out, done)
    copy.start()
    copy.wait()


def act_kernel(parts, out, held, done):
    half = parts.shape[2] // 2
    sums = parts[0].astype(F32)
    for i in range(1, 8):
        sums += parts[i].astype(F32)
    value, slope = gelu_pair(sums[:, :half])
    value = value.astype(BF16)
    slope = (sums[:, half:] * slope).astype(BF16)
    for i in range(8):
        held[i, :, :half] = value
        held[i, :, half:] = slope
    copy = pltpu.make_async_copy(held, out, done)
    copy.start()
    copy.wait()


def sum_kernel(terms, out, held, done):
    sums = terms[0].astype(F32)
    for i in range(1, 4):
        sums += terms[i].astype(F32)
    width = sums.shape[1] // 2
    for a in range(2):
        held[:, a] = sums[:, a * width : (a + 1) * width].reshape(8, 8, width).astype(BF16)
    copy = pltpu.make_async_copy(held, out, done)
    copy.start()
    copy.wait()


def forward_kernel(near, w00, w01, w10, w11, parts):
    width = w00.shape[1]
    for c, (own, other) in enumerate(((w00, w10), (w01, w11))):
        for j in range(2):
            rows, contract = slice(j * width, (j + 1) * width), j
            sums = dot(near[:, 2 * j * width : (2 * j + 1) * width], own[rows], 1, contract)
            sums += dot(near[:, (2 * j + 1) * width : (2 * j + 2) * width], other[rows], 1, contract)
            parts[:, (2 * j + c) * width : (2 * j + c + 1) * width] = sums.astype(BF16)


def terms_kernel(core, both, w00, w01, w10, w11, terms, held, done):
    width = w00.shape[1]
    d = [both[:, (2 + c) * width : (3 + c) * width] for c in range(2)]
    slabs = [
        dot(d[0], row[0][:width], 1, 1) + dot(d[1], row[1][:width], 1, 1)
        for row in ((w00, w01), (w10, w11))
    ]
    for a in range(2):
        chosen = jnp.where(core[0] == a, slabs[0], slabs[1]).astype(BF16)
        held[:, :, a * width : (a + 1) * width] = chosen.reshape(4, 64, width)
    copy = pltpu.make_async_copy(held, terms, done)
    copy.start()
    copy.wait()


def two_grads(near, both, slab, column):
    width = both.shape[1] // 4
    part = lambda ref, i: ref[:, i * width : (i + 1) * width]
    return (
        dot(part(near, slab), part(both, 2 + column), 0, 0),
        dot(part(both, column), part(near, 2 + slab), 0, 0),
    )


def send_kernel(near, both, out0, out1, out2, held0, held1, held2, done0, done1, done2):
    width = out0.shape[1]
    copies = []
    for (slab, column), out, held, done in zip(
        WAYS, (out0, out1, out2), (held0, held1, held2), (done0, done1, done2)
    ):
        first, second = two_grads(near, both, slab, column)
        held[:width] = first.astype(BF16)
        held[width:] = second.astype(BF16)
        copies.append(pltpu.make_async_copy(held, out, done))
        copies[-1].start()
    for copy in copies:
        copy.wait()


def grads_kernel(near, both, came0, came1, came2, grad_first, grad_second):
    width = grad_first.shape[0]
    first, second = two_grads(near, both, 0, 0)
    for came in (came0, came1, came2):
        first += came[:width].astype(F32)
        second += came[width:].astype(F32)
    grad_first[...] = first
    grad_second[...] = second


def local(inputs, out_grad, w_first, w_second):
    rows, width = inputs.shape
    half = rows // 2
    core = lax.axis_index("core")

    packed = jnp.concatenate([w_first, w_second])
    held = [packed, flip(packed, 0, 1), flip(packed, 1, 0), flip(packed, 1, 1)]

    blocks = [((8, 2, 2, half, width), BF16)]
    (pair,) = call(spread_kernel, blocks, inputs, out_grad, far=1, limit=56)
    far = exchange_far(pair.reshape(16, 2, half, width)).reshape(8, 2, 2, half, width)
    far = far.transpose(2, 1, 0, 3, 4).reshape(2, 2, 8 * half, width)
    own_in, own_grad = [jnp.where(core == 0, f[0], f[1]) for f in far]
    other_in, other_grad = [jnp.where(core == 0, f[1], f[0]) for f in far]
    far = jnp.concatenate([own_in, other_in, own_grad, other_grad], axis=1)

    near = lax.all_gather(far, RING, axis=0, axis_index_groups=FOLD, tiled=True)
    tokens = near.shape[0]
    (parts,) = call(forward_kernel, [((tokens, 4 * width), BF16)], near, *held)
    parts = exchange(parts.reshape(8, tokens // 8, 4 * width), PLANE)
    (both,) = call(act_kernel, [(parts.shape, BF16)], parts, far=1)
    both = exchange(both, PLANE)
    both = both.reshape(tokens, 4 * width)

    (terms,) = call(
        terms_kernel,
        [((4, 8 * half, 2 * width), BF16)],
        core.reshape(1).astype(jnp.int32),
        both,
        *held,
        scalars=1,
        far=1,
        cost=BOUND,
    )
    blocks = [((2 * width, width), BF16)] * 3
    sent = call(send_kernel, blocks, near, both, far=3, cost=BOUND)
    came = [flip(block, *way) for block, way in zip(sent, WAYS)]
    terms = lax.all_to_all(terms, RING, 0, 0, axis_index_groups=FOLD, tiled=False)
    (terms,) = call(sum_kernel, [((8, 2, half, width), BF16)], terms, far=1)
    terms = exchange_far(terms.reshape(16, half, width)).reshape(8, 2, half, width)
    d_input = jnp.sum(terms.astype(F32), axis=0).astype(BF16).reshape(rows, width)
    grad_first, grad_second = call(grads_kernel, [((width, width), F32)] * 2, near, both, *came, cost=COST)
    return (d_input, grad_first, grad_second)


def solution(mesh):
    fine = Mesh(mesh.devices.reshape(2, 4, 2, 2, 8, 4), ("xh", "y", "core", "xl", "zh", "zl"))
    row, col = ("xh", "y", "core"), ("xl", "zh", "zl")
    placed = (P(col, row), P(col, row), P(row, col), P(col, row))
    return jax.shard_map(
        local,
        mesh=fine,
        in_specs=placed,
        out_specs=(P(col, row), P(row, col), P(col, row)),
        check_vma=False,
    )
```

```python
import math

import jax
import jax.numpy as jnp
from jax import lax
from jax.experimental import pallas as pl
from jax.experimental.pallas import tpu as pltpu
from jax.sharding import Mesh, PartitionSpec as P

QUAD = ("core", "xl")
PLANE = ("xh", "y")
LIMIT = 16
COST = pl.CostEstimate(flops=30 * 10**9, bytes_accessed=2**22, transcendentals=0)
BOUND = pl.CostEstimate(flops=10**9, bytes_accessed=2**10, transcendentals=0)
SPAN = ("core", "zh", "zl")
RING = ("zh", "zl")
FOLD = [[z * 4 + low for low in (1, 0, 2, 3)] for z in range(8)]
WAYS = ((1, 1), (0, 1), (1, 0))
F32 = jnp.float32
BF16 = jnp.bfloat16


def gelu_pair(pre):
    cdf = 0.5 * (1.0 + jax.scipy.special.erf(pre / math.sqrt(2.0)))
    dens = jnp.exp(-0.5 * pre * pre) / math.sqrt(2.0 * math.pi)
    return (pre * cdf, cdf + pre * dens)


def exchange(blocks, axes):
    return lax.all_to_all(blocks, axes, 0, 0, tiled=False)


def exchange_far(blocks):
    groups = [
        [c * 32 + z * 4 + low for z in (4, 0, 1, 7, 2, 6, 3, 5) for c in range(2)] for low in range(4)
    ]
    return lax.all_to_all(blocks, SPAN, 0, 0, axis_index_groups=groups, tiled=False)


def flip(block, slab, column):
    return lax.ppermute(block, QUAD, [(i, i ^ (2 * slab + column)) for i in range(4)])


def dot(a, b, ca, cb):
    return lax.dot_general(a, b, (((ca,), (cb,)), ((), ())), preferred_element_type=F32)


def call(kernel, outs, *operands, scalars=0, far=0, cost=None, limit=LIMIT):
    specs = [pl.BlockSpec(memory_space=pltpu.SMEM)] * scalars
    specs += [pl.BlockSpec(memory_space=pltpu.VMEM)] * (len(operands) - scalars)
    out_specs = [pl.BlockSpec(memory_space=pltpu.HBM)] * far
    out_specs += [pl.BlockSpec(memory_space=pltpu.VMEM)] * (len(outs) - far)
    scratch = [pltpu.VMEM(shape, kind) for shape, kind in outs[:far]]
    scratch += [pltpu.SemaphoreType.DMA] * far
    return pl.pallas_call(
        kernel,
        out_shape=[jax.ShapeDtypeStruct(shape, kind) for shape, kind in outs],
        in_specs=specs,
        out_specs=out_specs,
        scratch_shapes=scratch,
        cost_estimate=cost,
        compiler_params=pltpu.CompilerParams(vmem_limit_bytes=limit * 2**20),
    )(*operands)


def spread_kernel(inputs, out_grad, out, held, done):
    half = inputs.shape[0] // 2
    for i, block in enumerate((inputs, out_grad)):
        wide = block[...].astype(F32)
        for c in range(2):
            piece = wide[c * half : (c + 1) * half].astype(BF16)
            for k in range(8):
                held[k, c, i] = piece
    copy = pltpu.make_async_copy(held, out, done)
    copy.start()
    copy.wait()


def act_kernel(parts, out, held, done):
    half = parts.shape[2] // 2
    sums = parts[0].astype(F32)
    for i in range(1, 8):
        sums += parts[i].astype(F32)
    value, slope = gelu_pair(sums[:, :half])
    value = value.astype(BF16)
    slope = (sums[:, half:] * slope).astype(BF16)
    for i in range(8):
        held[i, :, :half] = value
        held[i, :, half:] = slope
    copy = pltpu.make_async_copy(held, out, done)
    copy.start()
    copy.wait()


def sum_kernel(terms, out, held, done):
    sums = terms[0].astype(F32)
    for i in range(1, 4):
        sums += terms[i].astype(F32)
    width = sums.shape[1] // 2
    for a in range(2):
        held[:, a] = sums[:, a * width : (a + 1) * width].reshape(8, 8, width).astype(BF16)
    copy = pltpu.make_async_copy(held, out, done)
    copy.start()
    copy.wait()


def forward_kernel(near, w00, w01, w10, w11, parts):
    width = w00.shape[1]
    for c, (own, other) in enumerate(((w00, w10), (w01, w11))):
        for j in range(2):
            rows, contract = slice(j * width, (j + 1) * width), j
            sums = dot(near[:, 2 * j * width : (2 * j + 1) * width], own[rows], 1, contract)
            sums += dot(near[:, (2 * j + 1) * width : (2 * j + 2) * width], other[rows], 1, contract)
            parts[:, (2 * j + c) * width : (2 * j + c + 1) * width] = sums.astype(BF16)


def terms_kernel(core, both, w00, w01, w10, w11, terms):
    width = w00.shape[1]
    d = [both[:, (2 + c) * width : (3 + c) * width] for c in range(2)]
    slabs = [
        dot(d[0], row[0][:width], 1, 1) + dot(d[1], row[1][:width], 1, 1)
        for row in ((w00, w01), (w10, w11))
    ]
    for a in range(2):
        chosen = jnp.where(core[0] == a, slabs[0], slabs[1]).astype(BF16)
        terms[:, :, a * width : (a + 1) * width] = chosen.reshape(4, 64, width)


def two_grads(near, both, slab, column):
    width = both.shape[1] // 4
    part = lambda ref, i: ref[:, i * width : (i + 1) * width]
    return (
        dot(part(near, slab), part(both, 2 + column), 0, 0),
        dot(part(both, column), part(near, 2 + slab), 0, 0),
    )


def send_kernel(near, both, out0, out1, out2, held0, held1, held2, done0, done1, done2):
    width = out0.shape[1]
    copies = []
    for (slab, column), out, held, done in zip(
        WAYS, (out0, out1, out2), (held0, held1, held2), (done0, done1, done2)
    ):
        first, second = two_grads(near, both, slab, column)
        held[:width] = first.astype(BF16)
        held[width:] = second.astype(BF16)
        copies.append(pltpu.make_async_copy(held, out, done))
        copies[-1].start()
    for copy in copies:
        copy.wait()


def grads_kernel(near, both, came0, came1, came2, grad_first, grad_second):
    width = grad_first.shape[0]
    first, second = two_grads(near, both, 0, 0)
    for came in (came0, came1, came2):
        first += came[:width].astype(F32)
        second += came[width:].astype(F32)
    grad_first[...] = first
    grad_second[...] = second


def local(inputs, out_grad, w_first, w_second):
    rows, width = inputs.shape
    half = rows // 2
    core = lax.axis_index("core")

    packed = jnp.concatenate([w_first, w_second])
    held = [packed, flip(packed, 0, 1), flip(packed, 1, 0), flip(packed, 1, 1)]

    blocks = [((8, 2, 2, half, width), BF16)]
    (pair,) = call(spread_kernel, blocks, inputs, out_grad, far=1, limit=56)
    far = exchange_far(pair.reshape(16, 2, half, width)).reshape(8, 2, 2, half, width)
    far = far.transpose(2, 1, 0, 3, 4).reshape(2, 2, 8 * half, width)
    own_in, own_grad = [jnp.where(core == 0, f[0], f[1]) for f in far]
    other_in, other_grad = [jnp.where(core == 0, f[1], f[0]) for f in far]
    far = jnp.concatenate([own_in, other_in, own_grad, other_grad], axis=1)

    near = lax.all_gather(far, RING, axis=0, axis_index_groups=FOLD, tiled=True)
    tokens = near.shape[0]
    (parts,) = call(forward_kernel, [((tokens, 4 * width), BF16)], near, *held)
    parts = exchange(parts.reshape(8, tokens // 8, 4 * width), PLANE)
    (both,) = call(act_kernel, [(parts.shape, BF16)], parts, far=1)
    both = exchange(both, PLANE)
    both = both.reshape(tokens, 4 * width)

    (terms,) = call(
        terms_kernel,
        [((4, 8 * half, 2 * width), BF16)],
        core.reshape(1).astype(jnp.int32),
        both,
        *held,
        scalars=1,
        cost=BOUND,
    )
    blocks = [((2 * width, width), BF16)] * 3
    sent = call(send_kernel, blocks, near, both, far=3, cost=BOUND)
    came = [flip(block, *way) for block, way in zip(sent, WAYS)]
    terms = lax.all_to_all(terms, RING, 0, 0, axis_index_groups=FOLD, tiled=False)
    (terms,) = call(sum_kernel, [((8, 2, half, width), BF16)], terms, far=1)
    terms = exchange_far(terms.reshape(16, half, width)).reshape(8, 2, half, width)
    d_input = jnp.sum(terms.astype(F32), axis=0).astype(BF16).reshape(rows, width)
    grad_first, grad_second = call(grads_kernel, [((width, width), F32)] * 2, near, both, *came, cost=COST)
    return (d_input, grad_first, grad_second)


def solution(mesh):
    fine = Mesh(mesh.devices.reshape(2, 4, 2, 2, 8, 4), ("xh", "y", "core", "xl", "zh", "zl"))
    row, col = ("xh", "y", "core"), ("xl", "zh", "zl")
    placed = (P(col, row), P(col, row), P(row, col), P(col, row))
    return jax.shard_map(
        local,
        mesh=fine,
        in_specs=placed,
        out_specs=(P(col, row), P(row, col), P(col, row)),
        check_vma=False,
    )
```
